512 devices in a mesh: replica: 32 (over y_lo, z), fsdp: 16 (over x, y_hi, core).
Axes of the slice: x: 4, y: 8 (y_hi: 2, y_lo: 4; y = y_hi * 4 + y_lo), z: 8, core: 2. Of those that a mesh axis runs over, the one named last changes fastest.
Arguments:
- activations: bfloat16 [131072, 4608], P(('replica', 'fsdp')), may hold values from -6 to 6
- base_master: float32 [4608, 1024], P(('fsdp', 'replica')), may hold values from -6 to 6
- momentum: float32 [4608, 1024], P(('fsdp', 'replica')), may hold values from -4 to 4
- inner_weights: bfloat16 [32, 4608, 1024], P('replica', 'fsdp'), may hold values from -6 to 6
Outputs:
- keys: bfloat16 [131072, 1024], P(('replica', 'fsdp'))
- base_out: float32 [4608, 1024], P(('fsdp', 'replica'))
- momentum_out: float32 [4608, 1024], P(('fsdp', 'replica'))
The draws below stay inside these ranges and needn't reach their ends.
All inputs are finite; a program needn't handle non-finite values.
Results may differ from the reference program's by a relative error of at most 0.024.
Values may be sent and summed in bfloat16 or wider, within the bound.
No kernel may reach another device: no remote copies, remote signals or barrier semaphores. Data moves between devices by JAX's collectives and lax.ppermute only.
A program may use at most 64 MiB of HBM per device.

```python
import jax
import jax.numpy as jnp
from jax import lax

D = 4608
KW = 1024
BLK = 128
REPLICAS = 32
TOKENS = 131072


def raised(values, rng, source, target, parts, factor):
    def block_of(dim):
        return (jnp.arange(values.shape[dim]) // (values.shape[dim] // parts)).reshape((-1,) + (1,) * (values.ndim - 1 - dim))

    one_side = jax.random.permutation(rng, parts)[block_of(target)]
    far = (block_of(target) + parts // 2) % parts
    return jnp.where((block_of(source) == one_side) | (block_of(source) == far), factor * values, values)


def shard_levels(key, dims, split, least, top_value):
    loudness = 1.0
    for position, shards_of in split:
        steps = jax.random.uniform(jax.random.fold_in(jax.random.fold_in(key, 6), position), (shards_of,), jnp.float32, least / len(split), top_value / len(split))
        loudness = loudness * jnp.repeat(jnp.exp(steps), dims[position] // shards_of).reshape((-1,) + (1,) * (len(dims) - 1 - position))
    return loudness


def normal_values(stream_key, extent, width, reach, cuts=(), held_as=jnp.bfloat16):
    level = shard_levels(stream_key, extent, cuts, -0.22, 0.18) if cuts else 1.0
    values = jax.random.normal(stream_key, extent, jnp.float32) * width * level
    return jnp.minimum(jnp.maximum(values, -reach), reach).astype(held_as)


def gaussian_with(rng, dims, scale, limit, shards, heavy, kind=jnp.bfloat16):
    array = scale * jax.random.normal(rng, dims, jnp.float32)
    if shards:
        array = array * shard_levels(rng, dims, shards, -0.22, 0.18)
    return jnp.clip(raised(array, jax.random.fold_in(rng, 3), *heavy), -limit, limit).astype(kind)


def setup_inputs(seed: int = 0) -> dict:
    streams_of = jax.random.split(jax.random.key(seed), 5)
    activations = normal_values(streams_of[0], (TOKENS, D), 1.0, 6.0, ((0, 512),))
    base_master = normal_values(streams_of[1], (D, KW), 1.0, 6.0, ((0, 512),), jnp.float32)
    momentum = normal_values(streams_of[2], (D, KW), 0.5, 4.0, ((0, 512),), jnp.float32)
    inner_weights = gaussian_with(streams_of[3], (REPLICAS, D, KW), 1.0, 6.0, ((0, 32), (1, 16)), (0, 1, 32, 2.75))
    return dict(activations=activations, base_master=base_master, momentum=momentum, inner_weights=inner_weights)


def encode(delta):
    blocks = delta.reshape(delta.shape[0], delta.shape[1] // BLK, BLK)
    largest = jnp.max(jnp.abs(blocks), axis=-1, keepdims=True)
    scales = (largest + 1e-6) / 448.0
    coded = (blocks / scales).astype(jnp.bfloat16)
    return coded, scales


def reference(activations, base_master, momentum, inner_weights):
    def add_one(total, inner_one):
        delta = base_master - inner_one.astype(jnp.float32)
        coded, scales = encode(delta)
        decoded = coded.astype(jnp.float32) * scales
        return total + decoded.reshape(D, KW), None

    total, unused = lax.scan(add_one, jnp.zeros((D, KW), jnp.float32), inner_weights)
    outer_grad = total / REPLICAS
    momentum_out = 0.9 * momentum + outer_grad
    base_out = base_master - 0.7 * (outer_grad + 0.9 * momentum_out)
    fragment = base_out.astype(jnp.bfloat16)
    keys = jnp.dot(activations, fragment, preferred_element_type=jnp.float32) * (D ** -0.5)
    return keys.astype(jnp.bfloat16), base_out, momentum_out
```

```python
import jax
import jax.numpy as jnp
from jax import lax
from jax.experimental import pallas as pl
from jax.experimental.pallas import tpu as pltpu
from jax.sharding import Mesh, PartitionSpec as P

D = 4608
BLK = 128
AXES = ("yl", "z", "x", "yh", "c")
SIZES = (4, 8, 4, 2, 2)
REPLICAS = 32
ROWS = ("yh", "yl", "z")


def outer_kernel(inner_ref, base_ref, mom_ref, base_out_ref, mom_out_ref, frag_ref):
    base = base_ref[...]
    total = jnp.zeros_like(base)
    for r in range(REPLICAS):
        delta = base - inner_ref[r].astype(jnp.float32)
        largest = jnp.max(jnp.abs(delta), axis=-1, keepdims=True)
        scales = (largest + 1e-06) / 448.0
        coded = (delta / scales).astype(jnp.bfloat16)
        total = total + coded.astype(jnp.float32) * scales
    outer_grad = total / REPLICAS
    momentum_out = 0.9 * mom_ref[...] + outer_grad
    base_out = base - 0.7 * (outer_grad + 0.9 * momentum_out)
    mom_out_ref[...] = momentum_out
    base_out_ref[...] = base_out
    frag_ref[...] = base_out.astype(jnp.bfloat16)


def outer_step(got, base, mom):
    n = base.shape[0]
    f32 = jax.ShapeDtypeStruct((n, BLK), jnp.float32)
    return pl.pallas_call(
        outer_kernel,
        out_shape=(f32, f32, jax.ShapeDtypeStruct((n, BLK), jnp.bfloat16)),
        name="outer_step",
    )(got, base, mom)


def shift(v, axis, by):
    n = lax.axis_size(axis)
    return lax.ppermute(v, axis, [(i, (i + by) % n) for i in range(n)])


def body(activations, base_master, momentum, inner_weights):
    owned, width = base_master.shape
    nx = lax.axis_size("x")
    x = lax.axis_index("x")
    c = lax.axis_index("c")
    flat = owned * width // BLK
    depth = activations.shape[1] // nx

    got = lax.all_to_all(
        inner_weights.reshape(REPLICAS, flat, BLK), ("yl", "z"), split_axis=0, concat_axis=0, tiled=True
    )

    def columns(by):
        return lax.dynamic_slice_in_dim(activations, lax.rem(x + (by + nx), nx) * depth, depth, axis=1)

    acts = {by: shift(columns(by), "x", by) for by in (2, 1, -1)}
    got, acts[1], acts[-1] = lax.optimization_barrier((got, acts[1], acts[-1]))

    base_flat, mom_flat, frag = outer_step(
        got, base_master.reshape(flat, BLK), momentum.reshape(flat, BLK)
    )
    pieces = 64
    mine = lax.all_to_all(
        jnp.broadcast_to(frag[None], (pieces, flat, BLK)), ROWS, split_axis=0, concat_axis=0, tiled=True
    )
    mine, acts[2] = lax.optimization_barrier((mine, acts[2]))
    mine = mine.reshape(2, REPLICAS * owned, width)
    other = shift(mine, "c", 1)
    first = jnp.where(c == 0, mine, other)
    second = jnp.where(c == 0, other, mine)
    rows = jnp.stack([first, second], axis=1).reshape(depth, width)

    total = jnp.dot(columns(0), rows, preferred_element_type=jnp.float32)
    for by in (2, 1, -1):
        part = jnp.dot(acts[by], rows, preferred_element_type=jnp.float32).astype(jnp.bfloat16)
        total = total + shift(part, "x", -by).astype(jnp.float32)
    keys = (total * D ** (-0.5)).astype(jnp.bfloat16)
    return keys, base_flat.reshape(owned, width), mom_flat.reshape(owned, width)


def solution(mesh):
    fine = Mesh(mesh.devices.reshape(SIZES), AXES)
    tokens = P(AXES, None)
    owned = P(("x", "yh", "c", "yl", "z"), None)
    return jax.shard_map(
        body,
        mesh=fine,
        in_specs=(tokens, owned, owned, P(("yl", "z"), ("x", "yh", "c"), None)),
        out_specs=(tokens, owned, owned),
        check_vma=False,
    )
```

```python
import jax
import jax.numpy as jnp
from jax import lax
from jax.experimental import pallas as pl
from jax.experimental.pallas import tpu as pltpu
from jax.sharding import Mesh, PartitionSpec as P

D = 4608
BLK = 128
AXES = ("yl", "z", "x", "yh", "c")
SIZES = (4, 8, 4, 2, 2)
REPLICAS = 32
CHIPS = 64
ROWS = ("yh", "yl", "z")


def outer_kernel(inner_ref, base_ref, mom_ref, base_out_ref, mom_out_ref, frag_ref):
    base = base_ref[...]
    total = jnp.zeros_like(base)
    for r in range(REPLICAS):
        delta = base - inner_ref[r].astype(jnp.float32)
        largest = jnp.max(jnp.abs(delta), axis=-1, keepdims=True)
        scales = (largest + 1e-06) / 448.0
        coded = (delta / scales).astype(jnp.bfloat16)
        total = total + coded.astype(jnp.float32) * scales
    outer_grad = total / REPLICAS
    momentum_out = 0.9 * mom_ref[...] + outer_grad
    base_out = base - 0.7 * (outer_grad + 0.9 * momentum_out)
    mom_out_ref[...] = momentum_out
    base_out_ref[...] = base_out
    frag = base_out.astype(jnp.bfloat16)
    for i in range(CHIPS):
        frag_ref[i] = frag


def outer_step(got, base, mom):
    n = base.shape[0]
    f32 = jax.ShapeDtypeStruct((n, BLK), jnp.float32)
    return pl.pallas_call(
        outer_kernel,
        out_shape=(f32, f32, jax.ShapeDtypeStruct((CHIPS, n, BLK), jnp.bfloat16)),
        name="outer_step",
    )(got, base, mom)


def shift(v, axis, by):
    n = lax.axis_size(axis)
    return lax.ppermute(v, axis, [(i, (i + by) % n) for i in range(n)])


def body(activations, base_master, momentum, inner_weights):
    owned, width = base_master.shape
    nx = lax.axis_size("x")
    x = lax.axis_index("x")
    c = lax.axis_index("c")
    flat = owned * width // BLK
    depth = activations.shape[1] // nx

    got = lax.all_to_all(
        inner_weights.reshape(REPLICAS, flat, BLK), ("yl", "z"), split_axis=0, concat_axis=0, tiled=True
    )

    def columns(by):
        return lax.dynamic_slice_in_dim(activations, lax.rem(x + (by + nx), nx) * depth, depth, axis=1)

    acts = {by: shift(columns(by), "x", by) for by in (2, 1, -1)}

    base_flat, mom_flat, copies = outer_step(
        got, base_master.reshape(flat, BLK), momentum.reshape(flat, BLK)
    )
    copies, acts[1], acts[-1] = lax.optimization_barrier((copies, acts[1], acts[-1]))
    mine = lax.all_to_all(copies, ROWS, split_axis=0, concat_axis=0, tiled=True)
    mine, acts[2] = lax.optimization_barrier((mine, acts[2]))
    mine = mine.reshape(2, REPLICAS * owned, width)
    other = shift(mine, "c", 1)
    first = jnp.where(c == 0, mine, other)
    second = jnp.where(c == 0, other, mine)
    rows = jnp.stack([first, second], axis=1).reshape(depth, width)

    total = jnp.dot(columns(0), rows, preferred_element_type=jnp.float32)
    for by in (2, 1, -1):
        part = jnp.dot(acts[by], rows, preferred_element_type=jnp.float32).astype(jnp.bfloat16)
        total = total + shift(part, "x", -by).astype(jnp.float32)
    keys = (total * D ** (-0.5)).astype(jnp.bfloat16)
    return keys, base_flat.reshape(owned, width), mom_flat.reshape(owned, width)


def solution(mesh):
    fine = Mesh(mesh.devices.reshape(SIZES), AXES)
    tokens = P(AXES, None)
    owned = P(("x", "yh", "c", "yl", "z"), None)
    return jax.shard_map(
        body,
        mesh=fine,
        in_specs=(tokens, owned, owned, P(("yl", "z"), ("x", "yh", "c"), None)),
        out_specs=(tokens, owned, owned),
        check_vma=False,
    )
```

```python
import jax
import jax.numpy as jnp
from jax import lax
from jax.experimental import pallas as pl
from jax.experimental.pallas import tpu as pltpu
from jax.sharding import Mesh, PartitionSpec as P

D = 4608
BLK = 128
AXES = ("yl", "z", "x", "yh", "c")
SIZES = (4, 8, 4, 2, 2)
REPLICAS = 32
CHIPS = 64
ROWS = ("yh", "yl", "z")


def outer_kernel(inner_ref, base_ref, mom_ref, base_out_ref, mom_out_ref, frag_ref):
    base = base_ref[...]
    total = jnp.zeros_like(base)
    for r in range(REPLICAS):
        delta = base - inner_ref[r].astype(jnp.float32)
        largest = jnp.max(jnp.abs(delta), axis=-1, keepdims=True)
        scales = (largest + 1e-06) / 448.0
        coded = (delta / scales).astype(jnp.bfloat16)
        total = total + coded.astype(jnp.float32) * scales
    outer_grad = total / REPLICAS
    momentum_out = 0.9 * mom_ref[...] + outer_grad
    base_out = base - 0.7 * (outer_grad + 0.9 * momentum_out)
    mom_out_ref[...] = momentum_out
    base_out_ref[...] = base_out
    frag = base_out.astype(jnp.bfloat16)
    for i in range(CHIPS):
        frag_ref[i] = frag


def outer_step(got, base, mom):
    n = base.shape[0]
    f32 = jax.ShapeDtypeStruct((n, BLK), jnp.float32)
    return pl.pallas_call(
        outer_kernel,
        out_shape=(f32, f32, jax.ShapeDtypeStruct((CHIPS, n, BLK), jnp.bfloat16)),
        compiler_params=pltpu.CompilerParams(vmem_limit_bytes=8 * 2**20),
        name="outer_step",
    )(got, base, mom)


def sum_kernel(own_ref, *refs):
    *part_refs, keys_ref = refs
    total = own_ref[...]
    for part_ref in part_refs:
        total = total + part_ref[...].astype(jnp.float32)
    keys_ref[...] = (total * D ** (-0.5)).astype(jnp.bfloat16)


def sum_parts(own, parts):
    return pl.pallas_call(
        sum_kernel,
        out_shape=jax.ShapeDtypeStruct(own.shape, jnp.bfloat16),
        compiler_params=pltpu.CompilerParams(vmem_limit_bytes=8 * 2**20),
        name="sum_parts",
    )(own, *parts)


def shift(v, axis, by):
    n = lax.axis_size(axis)
    return lax.ppermute(v, axis, [(i, (i + by) % n) for i in range(n)])


def body(activations, base_master, momentum, inner_weights):
    owned, width = base_master.shape
    nx = lax.axis_size("x")
    x = lax.axis_index("x")
    c = lax.axis_index("c")
    flat = owned * width // BLK
    depth = activations.shape[1] // nx

    got = lax.all_to_all(
        inner_weights.reshape(REPLICAS, flat, BLK), ("yl", "z"), split_axis=0, concat_axis=0, tiled=True
    )

    def columns(by):
        return lax.dynamic_slice_in_dim(activations, lax.rem(x + (by + nx), nx) * depth, depth, axis=1)

    acts = {by: shift(columns(by), "x", by) for by in (2, 1, -1)}

    base_flat, mom_flat, copies = outer_step(
        got, base_master.reshape(flat, BLK), momentum.reshape(flat, BLK)
    )
    copies, acts[1] = lax.optimization_barrier((copies, acts[1]))
    mine = lax.all_to_all(copies, ROWS, split_axis=0, concat_axis=0, tiled=True)
    mine, acts[2], acts[-1] = lax.optimization_barrier((mine, acts[2], acts[-1]))
    mine = mine.reshape(2, REPLICAS * owned, width)
    other = shift(mine, "c", 1)
    first = jnp.where(c == 0, mine, other)
    second = jnp.where(c == 0, other, mine)
    rows = jnp.stack([first, second], axis=1).reshape(depth, width)

    def product(a):
        return jnp.dot(a, rows, preferred_element_type=jnp.float32)

    far = product(acts[2]).astype(jnp.bfloat16)
    far, acts[1], acts[-1] = lax.optimization_barrier((far, acts[1], acts[-1]))
    own = product(columns(0))
    near = [shift(product(acts[by]).astype(jnp.bfloat16), "x", -by) for by in (1, -1)]
    own = own + shift(far, "x", -2).astype(jnp.float32)
    own, *near = lax.optimization_barrier((own, *near))
    keys = sum_parts(own, near)
    return keys, base_flat.reshape(owned, width), mom_flat.reshape(owned, width)


def solution(mesh):
    fine = Mesh(mesh.devices.reshape(SIZES), AXES)
    tokens = P(AXES, None)
    owned = P(("x", "yh", "c", "yl", "z"), None)
    return jax.shard_map(
        body,
        mesh=fine,
        in_specs=(tokens, owned, owned, P(("yl", "z"), ("x", "yh", "c"), None)),
        out_specs=(tokens, owned, owned),
        check_vma=False,
    )
```

```python
import jax
import jax.numpy as jnp
from jax import lax
from jax.experimental import pallas as pl
from jax.experimental.pallas import tpu as pltpu
from jax.sharding import Mesh, PartitionSpec as P

D = 4608
BLK = 128
AXES = ("yl", "z", "x", "yh", "c")
SIZES = (4, 8, 4, 2, 2)
REPLICAS = 32
CHIPS = 64
ROWS = ("yh", "z", "yl")


def outer_kernel(inner_ref, base_ref, mom_ref, base_out_ref, mom_out_ref, frag_ref):
    base = base_ref[...]
    total = jnp.zeros_like(base)
    for r in range(REPLICAS):
        delta = base - inner_ref[r].astype(jnp.float32)
        largest = jnp.max(jnp.abs(delta), axis=-1, keepdims=True)
        scales = (largest + 1e-06) / 448.0
        coded = (delta / scales).astype(jnp.bfloat16)
        total = total + coded.astype(jnp.float32) * scales
    outer_grad = total / REPLICAS
    momentum_out = 0.9 * mom_ref[...] + outer_grad
    base_out = base - 0.7 * (outer_grad + 0.9 * momentum_out)
    mom_out_ref[...] = momentum_out
    base_out_ref[...] = base_out
    frag = base_out.astype(jnp.bfloat16)
    for i in range(CHIPS):
        frag_ref[i] = frag


def outer_step(got, base, mom):
    n = base.shape[0]
    f32 = jax.ShapeDtypeStruct((n, BLK), jnp.float32)
    return pl.pallas_call(
        outer_kernel,
        out_shape=(f32, f32, jax.ShapeDtypeStruct((CHIPS, n, BLK), jnp.bfloat16)),
        compiler_params=pltpu.CompilerParams(vmem_limit_bytes=8 * 2**20),
        name="outer_step",
    )(got, base, mom)


def far_kernel(core_ref, mine_ref, other_ref, act_ref, part_ref, rows_ref):
    n = mine_ref.shape[1]
    c = core_ref[0]
    for h in range(2):
        rows_ref[pl.ds(pl.multiple_of((2 * h + c) * n, n), n), :] = mine_ref[h]
        rows_ref[pl.ds(pl.multiple_of((2 * h + 1 - c) * n, n), n), :] = other_ref[h]
    part_ref[...] = jnp.dot(act_ref[...], rows_ref[...], preferred_element_type=jnp.float32).astype(jnp.bfloat16)


def far_product(c, mine, other, act):
    width = mine.shape[2]
    whole = pl.BlockSpec(memory_space=pltpu.VMEM)
    return pl.pallas_call(
        far_kernel,
        in_specs=[pl.BlockSpec(memory_space=pltpu.SMEM), whole, whole, whole],
        out_specs=whole,
        out_shape=jax.ShapeDtypeStruct((act.shape[0], width), jnp.bfloat16),
        scratch_shapes=[pltpu.VMEM((act.shape[1], width), jnp.bfloat16)],
        compiler_params=pltpu.CompilerParams(vmem_limit_bytes=16 * 2**20),
        name="far_product",
    )(c.reshape(1), mine, other, act)


def sum_kernel(own_ref, *refs):
    *part_refs, keys_ref = refs
    total = own_ref[...]
    for part_ref in part_refs:
        total = total + part_ref[...].astype(jnp.float32)
    keys_ref[...] = (total * D ** (-0.5)).astype(jnp.bfloat16)


def sum_parts(own, parts):
    return pl.pallas_call(
        sum_kernel,
        out_shape=jax.ShapeDtypeStruct(own.shape, jnp.bfloat16),
        compiler_params=pltpu.CompilerParams(vmem_limit_bytes=8 * 2**20),
        name="sum_parts",
    )(own, *parts)


def shift(v, axis, by):
    n = lax.axis_size(axis)
    return lax.ppermute(v, axis, [(i, (i + by) % n) for i in range(n)])


def body(activations, base_master, momentum, inner_weights):
    owned, width = base_master.shape
    nx = lax.axis_size("x")
    x = lax.axis_index("x")
    c = lax.axis_index("c")
    flat = owned * width // BLK
    depth = activations.shape[1] // nx

    got = lax.all_to_all(
        inner_weights.reshape(REPLICAS, flat, BLK), ("yl", "z"), split_axis=0, concat_axis=0, tiled=True
    )

    def columns(by):
        return lax.dynamic_slice_in_dim(activations, lax.rem(x + (by + nx), nx) * depth, depth, axis=1)

    acts = {by: shift(columns(by), "x", by) for by in (2, 1, -1)}

    base_flat, mom_flat, copies = outer_step(
        got, base_master.reshape(flat, BLK), momentum.reshape(flat, BLK)
    )
    copies, acts[1] = lax.optimization_barrier((copies, acts[1]))
    mine = lax.all_to_all(copies, ROWS, split_axis=0, concat_axis=0, tiled=True)
    base_out, mom_out = base_flat.reshape(owned, width), mom_flat.reshape(owned, width)
    mine, acts[2], acts[-1], base_out, mom_out = lax.optimization_barrier(
        (mine, acts[2], acts[-1], base_out, mom_out)
    )
    mine = mine.reshape(2, 8, 4, flat, BLK).swapaxes(1, 2).reshape(2, REPLICAS * owned, width)
    other = shift(mine, "c", 1)
    far = far_product(c, mine, other, acts[2])
    first = jnp.where(c == 0, mine, other)
    second = jnp.where(c == 0, other, mine)
    rows = jnp.stack([first, second], axis=1).reshape(depth, width)

    def product(a):
        return jnp.dot(a, rows, preferred_element_type=jnp.float32)

    own = product(columns(0))
    near = [shift(product(acts[by]).astype(jnp.bfloat16), "x", -by) for by in (1, -1)]
    own = own + shift(far, "x", -2).astype(jnp.float32)
    own, *near = lax.optimization_barrier((own, *near))
    keys = sum_parts(own, near)
    return keys, base_out, mom_out


def solution(mesh):
    fine = Mesh(mesh.devices.reshape(SIZES), AXES)
    tokens = P(AXES, None)
    owned = P(("x", "yh", "c", "yl", "z"), None)
    return jax.shard_map(
        body,
        mesh=fine,
        in_specs=(tokens, owned, owned, P(("yl", "z"), ("x", "yh", "c"), None)),
        out_specs=(tokens, owned, owned),
        check_vma=False,
    )
```

```python
import jax
import jax.numpy as jnp
from jax import lax
from jax.experimental import pallas as pl
from jax.experimental.pallas import tpu as pltpu
from jax.sharding import Mesh, PartitionSpec as P

D = 4608
BLK = 128
AXES = ("yl", "z", "x", "yh", "c")
SIZES = (4, 8, 4, 2, 2)
REPLICAS = 32
CHIPS = 64
ROWS = ("yh", "z", "yl")


def outer_kernel(inner_ref, base_ref, mom_ref, base_out_ref, mom_out_ref, frag_ref):
    base = base_ref[...]
    total = jnp.zeros_like(base)
    for r in range(REPLICAS):
        delta = base - inner_ref[r].astype(jnp.float32)
        largest = jnp.max(jnp.abs(delta), axis=-1, keepdims=True)
        scales = (largest + 1e-06) / 448.0
        coded = (delta / scales).astype(jnp.bfloat16)
        total = total + coded.astype(jnp.float32) * scales
    outer_grad = total / REPLICAS
    momentum_out = 0.9 * mom_ref[...] + outer_grad
    base_out = base - 0.7 * (outer_grad + 0.9 * momentum_out)
    mom_out_ref[...] = momentum_out
    base_out_ref[...] = base_out
    frag = base_out.astype(jnp.bfloat16)
    for i in range(CHIPS):
        frag_ref[i] = frag


def outer_step(got, base, mom):
    n = base.shape[0]
    f32 = jax.ShapeDtypeStruct((n, BLK), jnp.float32)
    return pl.pallas_call(
        outer_kernel,
        out_shape=(f32, f32, jax.ShapeDtypeStruct((CHIPS, n, BLK), jnp.bfloat16)),
        compiler_params=pltpu.CompilerParams(vmem_limit_bytes=8 * 2**20),
        name="outer_step",
    )(got, base, mom)


def far_kernel(core_ref, mine_ref, other_ref, act_ref, part_ref, rows_ref):
    n = mine_ref.shape[1]
    c = core_ref[0]
    for h in range(2):
        rows_ref[pl.ds(pl.multiple_of((2 * h + c) * n, n), n), :] = mine_ref[h]
        rows_ref[pl.ds(pl.multiple_of((2 * h + 1 - c) * n, n), n), :] = other_ref[h]
    part_ref[...] = jnp.dot(act_ref[...], rows_ref[...], preferred_element_type=jnp.float32).astype(jnp.bfloat16)


def far_product(c, mine, other, act):
    width = mine.shape[2]
    whole = pl.BlockSpec(memory_space=pltpu.VMEM)
    return pl.pallas_call(
        far_kernel,
        in_specs=[pl.BlockSpec(memory_space=pltpu.SMEM), whole, whole, whole],
        out_specs=whole,
        out_shape=jax.ShapeDtypeStruct((act.shape[0], width), jnp.bfloat16),
        scratch_shapes=[pltpu.VMEM((act.shape[1], width), jnp.bfloat16)],
        compiler_params=pltpu.CompilerParams(vmem_limit_bytes=8 * 2**20),
        name="far_product",
    )(c.reshape(1), mine, other, act)


def sum_kernel(own_ref, *refs):
    *part_refs, keys_ref = refs
    total = own_ref[...]
    for part_ref in part_refs:
        total = total + part_ref[...].astype(jnp.float32)
    keys_ref[...] = (total * D ** (-0.5)).astype(jnp.bfloat16)


def sum_parts(own, parts):
    return pl.pallas_call(
        sum_kernel,
        out_shape=jax.ShapeDtypeStruct(own.shape, jnp.bfloat16),
        compiler_params=pltpu.CompilerParams(vmem_limit_bytes=8 * 2**20),
        name="sum_parts",
    )(own, *parts)


def shift(v, axis, by):
    n = lax.axis_size(axis)
    return lax.ppermute(v, axis, [(i, (i + by) % n) for i in range(n)])


def body(activations, base_master, momentum, inner_weights):
    owned, width = base_master.shape
    nx = lax.axis_size("x")
    x = lax.axis_index("x")
    c = lax.axis_index("c")
    flat = owned * width // BLK
    depth = activations.shape[1] // nx

    got = lax.all_to_all(
        inner_weights.reshape(REPLICAS, flat, BLK), ("yl", "z"), split_axis=0, concat_axis=0, tiled=True
    )

    def columns(by):
        return lax.dynamic_slice_in_dim(activations, lax.rem(x + (by + nx), nx) * depth, depth, axis=1)

    acts = {by: shift(columns(by), "x", by) for by in (2, 1, -1)}

    base_flat, mom_flat, copies = outer_step(
        got, base_master.reshape(flat, BLK), momentum.reshape(flat, BLK)
    )
    copies, acts[1] = lax.optimization_barrier((copies, acts[1]))
    mine = lax.all_to_all(copies, ROWS, split_axis=0, concat_axis=0, tiled=True)
    base_out, mom_out = base_flat.reshape(owned, width), mom_flat.reshape(owned, width)
    mine, acts[2], acts[-1], base_out, mom_out = lax.optimization_barrier(
        (mine, acts[2], acts[-1], base_out, mom_out)
    )
    mine = mine.reshape(2, 8, 4, flat, BLK).swapaxes(1, 2).reshape(2, REPLICAS * owned, width)
    other = shift(mine, "c", 1)
    far = far_product(c, mine, other, acts[2])
    first = jnp.where(c == 0, mine, other)
    second = jnp.where(c == 0, other, mine)
    rows = jnp.stack([first, second], axis=1).reshape(depth, width)

    def product(a):
        return jnp.dot(a, rows, preferred_element_type=jnp.float32)

    own = product(columns(0))
    near = [shift(product(acts[by]).astype(jnp.bfloat16), "x", -by) for by in (1, -1)]
    own = own + shift(far, "x", -2).astype(jnp.float32)
    own, *near = lax.optimization_barrier((own, *near))
    keys = sum_parts(own, near)
    return keys, base_out, mom_out


def solution(mesh):
    fine = Mesh(mesh.devices.reshape(SIZES), AXES)
    tokens = P(AXES, None)
    owned = P(("x", "yh", "c", "yl", "z"), None)
    return jax.shard_map(
        body,
        mesh=fine,
        in_specs=(tokens, owned, owned, P(("yl", "z"), ("x", "yh", "c"), None)),
        out_specs=(tokens, owned, owned),
        check_vma=False,
    )
```

```python
import jax
import jax.numpy as jnp
from jax import lax
from jax.experimental import pallas as pl
from jax.experimental.pallas import tpu as pltpu
from jax.sharding import Mesh, PartitionSpec as P

D = 4608
BLK = 128
AXES = ("yl", "z", "x", "yh", "c")
SIZES = (4, 8, 4, 2, 2)
REPLICAS = 32
CHIPS = 64
ROWS = ("yh", "z", "yl")


def outer_kernel(inner_ref, base_ref, mom_ref, base_out_ref, mom_out_ref, frag_ref):
    base = base_ref[...]
    total = jnp.zeros_like(base)
    for r in range(REPLICAS):
        delta = base - inner_ref[r].astype(jnp.float32)
        largest = jnp.max(jnp.abs(delta), axis=-1, keepdims=True)
        scales = (largest + 1e-06) / 448.0
        coded = (delta / scales).astype(jnp.bfloat16)
        total = total + coded.astype(jnp.float32) * scales
    outer_grad = total / REPLICAS
    momentum_out = 0.9 * mom_ref[...] + outer_grad
    base_out = base - 0.7 * (outer_grad + 0.9 * momentum_out)
    mom_out_ref[...] = momentum_out
    base_out_ref[...] = base_out
    frag = base_out.astype(jnp.bfloat16)
    for i in range(CHIPS):
        frag_ref[i] = frag


def outer_step(got, base, mom):
    n = base.shape[0]
    f32 = jax.ShapeDtypeStruct((n, BLK), jnp.float32)
    return pl.pallas_call(
        outer_kernel,
        out_shape=(f32, f32, jax.ShapeDtypeStruct((CHIPS, n, BLK), jnp.bfloat16)),
        compiler_params=pltpu.CompilerParams(vmem_limit_bytes=8 * 2**20),
        name="outer_step",
    )(got, base, mom)


def far_kernel(core_ref, mine_ref, other_ref, act_ref, part_ref, rows_ref):
    n = mine_ref.shape[1]
    c = core_ref[0]
    for h in range(2):
        rows_ref[pl.ds(pl.multiple_of((2 * h + c) * n, n), n), :] = mine_ref[h]
        rows_ref[pl.ds(pl.multiple_of((2 * h + 1 - c) * n, n), n), :] = other_ref[h]
    part_ref[...] = jnp.dot(act_ref[...], rows_ref[...], preferred_element_type=jnp.float32).astype(jnp.bfloat16)


def far_product(c, mine, other, act):
    width = mine.shape[2]
    whole = pl.BlockSpec(memory_space=pltpu.VMEM)
    return pl.pallas_call(
        far_kernel,
        in_specs=[pl.BlockSpec(memory_space=pltpu.SMEM), whole, whole, whole],
        out_specs=whole,
        out_shape=jax.ShapeDtypeStruct((act.shape[0], width), jnp.bfloat16),
        scratch_shapes=[pltpu.VMEM((act.shape[1], width), jnp.bfloat16)],
        compiler_params=pltpu.CompilerParams(vmem_limit_bytes=16 * 2**20),
        name="far_product",
    )(c.reshape(1), mine, other, act)


def sum_kernel(own_ref, *refs):
    *part_refs, keys_ref = refs
    total = own_ref[...]
    for part_ref in part_refs:
        total = total + part_ref[...].astype(jnp.float32)
    keys_ref[...] = (total * D ** (-0.5)).astype(jnp.bfloat16)


def sum_parts(own, parts):
    return pl.pallas_call(
        sum_kernel,
        out_shape=jax.ShapeDtypeStruct(own.shape, jnp.bfloat16),
        compiler_params=pltpu.CompilerParams(vmem_limit_bytes=8 * 2**20),
        name="sum_parts",
    )(own, *parts)


def shift(v, axis, by):
    n = lax.axis_size(axis)
    return lax.ppermute(v, axis, [(i, (i + by) % n) for i in range(n)])


def body(activations, base_master, momentum, inner_weights):
    owned, width = base_master.shape
    nx = lax.axis_size("x")
    x = lax.axis_index("x")
    c = lax.axis_index("c")
    flat = owned * width // BLK
    depth = activations.shape[1] // nx

    sent = inner_weights.reshape(4, 8, flat, BLK).swapaxes(0, 1).reshape(REPLICAS, flat, BLK)
    got = lax.all_to_all(sent, ("z", "yl"), split_axis=0, concat_axis=0, tiled=True)

    def columns(by):
        return lax.dynamic_slice_in_dim(activations, lax.rem(x + (by + nx), nx) * depth, depth, axis=1)

    acts = {by: shift(columns(by), "x", by) for by in (2, 1, -1)}

    base_flat, mom_flat, copies = outer_step(
        got, base_master.reshape(flat, BLK), momentum.reshape(flat, BLK)
    )
    copies, acts[1] = lax.optimization_barrier((copies, acts[1]))
    mine = lax.all_to_all(copies, ROWS, split_axis=0, concat_axis=0, tiled=True)
    base_out, mom_out = base_flat.reshape(owned, width), mom_flat.reshape(owned, width)
    mine, acts[2], acts[-1], base_out, mom_out = lax.optimization_barrier(
        (mine, acts[2], acts[-1], base_out, mom_out)
    )
    mine = mine.reshape(2, 8, 4, flat, BLK).swapaxes(1, 2).reshape(2, REPLICAS * owned, width)
    other = shift(mine, "c", 1)
    far = far_product(c, mine, other, acts[2])
    first = jnp.where(c == 0, mine, other)
    second = jnp.where(c == 0, other, mine)
    rows = jnp.stack([first, second], axis=1).reshape(depth, width)

    def product(a):
        return jnp.dot(a, rows, preferred_element_type=jnp.float32)

    own = product(columns(0))
    near = [shift(product(acts[by]).astype(jnp.bfloat16), "x", -by) for by in (1, -1)]
    own = own + shift(far, "x", -2).astype(jnp.float32)
    own, *near = lax.optimization_barrier((own, *near))
    keys = sum_parts(own, near)
    return keys, base_out, mom_out


def solution(mesh):
    fine = Mesh(mesh.devices.reshape(SIZES), AXES)
    tokens = P(AXES, None)
    owned = P(("x", "yh", "c", "yl", "z"), None)
    return jax.shard_map(
        body,
        mesh=fine,
        in_specs=(tokens, owned, owned, P(("yl", "z"), ("x", "yh", "c"), None)),
        out_specs=(tokens, owned, owned),
        check_vma=False,
    )
```
